32 devices in a mesh: dp: 2 (over x), ep: 16 (over z, y, core).
Axes of the slice: x: 2, y: 2, z: 4, core: 2. Of those that a mesh axis runs over, the one named last changes fastest.
Arguments:
- tokens: bfloat16 [4096, 2048], P(('dp', 'ep'))
- cotangent: bfloat16 [4096, 2048], P(('dp', 'ep'))
- expert_ids: int32 [4096, 8], P(('dp', 'ep')), may hold values from 0 to 15, all different within a row; in each aligned block of 128 rows (0 to 127, 128 to 255, ...) at most 72 rows name the same one
- route_weights: bfloat16 [4096, 8], P(('dp', 'ep')), may hold values from 0.029907227 to 0.3984375
- weights: bfloat16 [16, 3, 2048, 384], P('ep')
- first_moment: bfloat16 [16, 3, 2048, 384], P('ep', None, 'dp'), may hold values from -4 to 4
- second_moment: bfloat16 [16, 3, 2048, 384], P('ep', None, 'dp'), may hold values from 0.049804688 to 0.5
Outputs:
- token_grad: bfloat16 [4096, 2048], P(('dp', 'ep'))
- routing_grad: bfloat16 [4096, 8], P(('dp', 'ep'))
- new_first: bfloat16 [16, 3, 2048, 384], P('ep', None, 'dp')
- new_second: bfloat16 [16, 3, 2048, 384], P('ep', None, 'dp')
- update: bfloat16 [16, 3, 2048, 384], P('ep', None, 'dp')
The draws below stay inside these ranges and needn't reach their ends.
Inputs may be any that keep to these rules, and one draw needn't show every extreme that they name: `expert_ids`: among the 128 rows of one device no expert is named by more than 72 rows.
All inputs are finite; a program needn't handle non-finite values.
Results may differ from the reference program's by a relative error of at most 0.0057.
Values may be sent and summed in bfloat16 or wider, within the bound.
A program may use at most 128 MiB of HBM per device.

```python
import math
import jax
import jax.numpy as jnp
import numpy as np
from jax import lax

D = 2048
HID = 384
TOPK = 8
ADAM_STEP = 10
TOK_DEV = 128
EXPERTS = 16
CAP = 72
TOKENS = 4096


def draw_weights(key, part):
    key_base = jax.random.fold_in(key, 101)
    key_jitter = jax.random.fold_in(key, 202)
    expert = jnp.arange(EXPERTS, dtype=jnp.float32)
    ramp = 0.6 * 3.0 ** (expert / max(EXPERTS - 1, 1))
    jitter = jnp.exp(jax.random.uniform(key_jitter, (EXPERTS, 3), minval=-0.15, maxval=0.15))
    fanin = jnp.array([D ** (-0.5), D ** (-0.5), HID ** (-0.5)], jnp.float32)
    factor = ramp[:, None] * jitter * fanin[None, :]
    base = jnp.clip(jax.random.normal(key_base, (EXPERTS, 3, D, HID)), -4.0, 4.0)
    return (base * factor[:, :, None, None]).astype(jnp.bfloat16)


def rising_columns(key, salt):
    key_base = jax.random.fold_in(key, salt)
    key_jitter = jax.random.fold_in(key, salt + 7)
    key_sign = jax.random.fold_in(key, salt + 11)
    key_size = jax.random.fold_in(key, salt + 13)
    feature = jnp.arange(D, dtype=jnp.float32) / max(D - 1, 1)
    jitter = jnp.exp(jax.random.uniform(key_jitter, (D,), minval=-0.1, maxval=0.1))
    feature_sign = jax.random.rademacher(key_sign, (D,)).astype(jnp.float32)
    offset_size = jax.random.uniform(key_size, (D,), minval=0.5, maxval=1.5)
    column_scale = 0.6 * 3.0 ** feature * jitter
    base = jnp.clip(jax.random.normal(key_base, (TOKENS, D)), -4.0, 4.0)
    shared = 0.4 * offset_size * feature_sign
    return ((base + shared[None, :]) * column_scale[None, :]).astype(jnp.bfloat16)


def draw_tokens(key, part):
    return rising_columns(key, 303)


def draw_cotangent(key, part):
    return rising_columns(key, 404)


def shard_levels(key, dims, split, smallest, top_value):
    factor_of = 1.0
    for axis_at, parts in split:
        draws = jax.random.uniform(jax.random.fold_in(jax.random.fold_in(key, 6), axis_at), (parts,), jnp.float32, smallest / len(split), top_value / len(split))
        factor_of = factor_of * jnp.repeat(jnp.exp(draws), dims[axis_at] // parts).reshape((-1,) + (1,) * (len(dims) - 1 - axis_at))
    return factor_of


def routed_block(rng, own, number, rows, amount, top, limit, skew):
    ranking = jax.random.permutation(rng, amount)
    heavy_load, common = load_shares(amount, rows * top, limit, skew, True), load_shares(amount, rows * top, limit, skew, False)
    places = jnp.arange(amount)

    def named(tallies, turn):
        used = int((tallies > 0).sum())
        fixed = max(1, used // 4)
        moved = fixed + (places - fixed + turn * (used - fixed)) % max(1, amount - fixed)
        return jnp.zeros((amount,), jnp.int32).at[ranking[jnp.where(places < fixed, places, moved)]].set(jnp.asarray(tallies, jnp.int32))

    tallies = jnp.where(number % 4 == 0, named(heavy_load, number // 4), named(common, number - number // 4 - 1))
    mixed = jax.random.permutation(jax.random.fold_in(own, 3), amount)
    giver, taker = mixed[0:amount // 2 * 2:2], mixed[1:amount // 2 * 2:2]
    slack = jnp.minimum(tallies[giver] - 1, limit - tallies[taker]) // 2
    slack = jnp.where((giver == ranking[0]) | (taker == ranking[0]) | (tallies[taker] == 0), 0, jnp.maximum(slack, 0))
    moved = jax.random.randint(jax.random.fold_in(own, 4), (amount // 2,), 0, 1 << 20) % (slack + 1)
    tallies = tallies.at[giver].add(-moved).at[taker].add(moved)
    items = jnp.searchsorted(jnp.cumsum(tallies), jnp.arange(rows * top), side="right").astype(jnp.int32)
    listing = items.reshape(top, rows).T
    listing = listing[jax.random.permutation(jax.random.fold_in(own, 1), rows)]
    turn = jax.random.randint(jax.random.fold_in(own, 2), (rows, 1), 0, top)
    return jnp.take_along_axis(listing, (jnp.arange(top)[None, :] + turn) % top, axis=1)


def load_shares(amount, total, bound, skew, full):
    weights = [(1 << 20) // math.isqrt(rank ** skew) + 1 for rank in range(1, amount + 1)]
    largest = bound if full else min(bound, max(-(-total // amount), total * weights[0] // sum(weights)))
    least = 1 if total - largest >= amount - 1 else 0
    given, rest = [largest] + [least] * (amount - 1), total - largest - least * (amount - 1)
    while rest > 0:
        movable = [i for i in range(1, amount) if given[i] < largest] or [i for i in range(1, amount) if given[i] < bound]
        mass, budget = sum([weights[i] for i in movable]), rest
        for i in movable:
            more = min(bound - given[i], max(1, budget * weights[i] // mass), rest)
            given[i] = given[i] + more
            rest = rest - more
    return np.array(given)


def centred(own_key, shape, spread, bound, pieces=(), kind=jnp.bfloat16):
    factor_of = shard_levels(own_key, shape, pieces, -0.22, 0.18) if pieces else 1.0
    result = jax.random.normal(own_key, shape, jnp.float32) * spread * factor_of
    return jnp.minimum(jnp.maximum(result, -bound), bound).astype(kind)


def setup_inputs(seed: int = 0) -> dict:
    arg_keys = jax.random.split(jax.random.key(seed), 8)
    tokens = draw_tokens(jax.random.fold_in(arg_keys[7], 71), 0)
    cotangent = draw_cotangent(jax.random.fold_in(arg_keys[7], 71), 0)
    expert_ids_keys = jax.random.split(jax.random.fold_in(arg_keys[2], 1), TOKENS // TOK_DEV)
    expert_ids_turns = jax.random.permutation(jax.random.fold_in(arg_keys[2], 3), TOKENS // TOK_DEV)
    expert_ids = jax.vmap(lambda own, number: routed_block(jax.random.fold_in(arg_keys[2], 2), own, number, TOK_DEV, EXPERTS, TOPK, CAP, 1))(expert_ids_keys, expert_ids_turns).reshape((TOKENS, TOPK))
    route_weights = jnp.clip(jnp.exp(math.log(0.3984375) - 2.5894505 * jax.random.uniform(arg_keys[3], (TOKENS, TOPK), jnp.float32) ** shard_levels(arg_keys[3], (TOKENS, TOPK), ((0, 32),), -0.2, 0.2)), 0.029907227, 0.3984375).astype(jnp.bfloat16)
    weights = draw_weights(jax.random.fold_in(arg_keys[7], 71), 0)
    first_moment = centred(arg_keys[5], (EXPERTS, 3, D, HID), 0.3, 4.0, ((0, 16), (2, 2)))
    second_moment = jnp.clip(jnp.exp(math.log(0.5) - 2.306499 * jax.random.uniform(arg_keys[6], (EXPERTS, 3, D, HID), jnp.float32) ** shard_levels(arg_keys[6], (EXPERTS, 3, D, HID), ((0, 16), (2, 2)), -0.2, 0.2)), 0.049804688, 0.5).astype(jnp.bfloat16)
    return {"tokens": tokens, "cotangent": cotangent, "expert_ids": expert_ids, "route_weights": route_weights, "weights": weights, "first_moment": first_moment, "second_moment": second_moment}


def reference(tokens, cotangent, expert_ids, route_weights, weights, first_moment, second_moment):
    blocks_count = TOKENS // TOK_DEV
    pairs = TOK_DEV * TOPK
    sentinel = blocks_count * pairs
    ids_blocks = expert_ids.reshape(blocks_count, pairs)
    onehot = (ids_blocks[:, :, None] == jnp.arange(EXPERTS, dtype=jnp.int32)[None, None, :]).astype(jnp.int32)
    position = (lax.optimization_barrier(jnp.sum(jnp.cumsum(onehot, 1) * onehot, 2)) - 1).astype(jnp.int32)
    block_index = jnp.broadcast_to(jnp.arange(blocks_count, dtype=jnp.int32)[:, None], (blocks_count, pairs))
    flat_index = jnp.arange(sentinel, dtype=jnp.int32).reshape(blocks_count, pairs)
    table = jnp.full((EXPERTS, blocks_count, CAP), sentinel, jnp.int32).at[ids_blocks, block_index, position].set(flat_index)
    weight_flat = route_weights.reshape(-1)

    def per_expert(carry, inputs):
        expert_weights, expert_table = inputs
        slot_index = expert_table.reshape(-1)
        valid = slot_index < sentinel
        safe_index = jnp.where(valid, slot_index, 0).astype(jnp.int32)
        token_row = (safe_index // TOPK).astype(jnp.int32)
        rows_x = jnp.where(valid[:, None], tokens[token_row], jnp.zeros((), tokens.dtype))
        rows_cot = jnp.where(valid[:, None], cotangent[token_row], jnp.zeros((), cotangent.dtype))
        rows_weight = jnp.where(valid, weight_flat[safe_index].astype(jnp.float32), jnp.float32(0.0))
        w_gate = expert_weights[0]
        w_up = expert_weights[1]
        w_down = expert_weights[2]
        gate_val = jnp.dot(rows_x, w_gate, preferred_element_type=jnp.float32)
        up_val = jnp.dot(rows_x, w_up, preferred_element_type=jnp.float32)
        sigmoid_gate = jax.nn.sigmoid(gate_val)
        activated = gate_val * sigmoid_gate
        hidden = lax.optimization_barrier((activated * up_val).astype(jnp.bfloat16))
        back_val = jnp.dot(rows_cot, w_down, preferred_element_type=jnp.float32)
        route_part = lax.optimization_barrier(lax.optimization_barrier(jnp.sum(hidden.astype(jnp.float32) * back_val, 1)).astype(jnp.bfloat16))
        scaled = rows_weight[:, None] * back_val
        dgate = (scaled * up_val * sigmoid_gate * (1.0 + gate_val * (1.0 - sigmoid_gate))).astype(jnp.bfloat16)
        dup = (scaled * activated).astype(jnp.bfloat16)
        down_cot = (rows_weight[:, None] * rows_cot.astype(jnp.float32)).astype(jnp.bfloat16)
        slot_back = jnp.dot(dgate, w_gate.T, preferred_element_type=jnp.float32) + jnp.dot(dup, w_up.T, preferred_element_type=jnp.float32)
        slot_back = lax.optimization_barrier(slot_back.astype(jnp.bfloat16))
        grad_gate = jnp.dot(rows_x.T, dgate, preferred_element_type=jnp.float32)
        grad_up = jnp.dot(rows_x.T, dup, preferred_element_type=jnp.float32)
        grad_down = jnp.dot(down_cot.T, hidden, preferred_element_type=jnp.float32)
        token_acc = carry[0].at[jnp.where(valid, token_row, TOKENS).astype(jnp.int32)].add(slot_back.astype(jnp.float32), mode='drop')
        route_acc = carry[1].at[jnp.where(valid, slot_index, sentinel).astype(jnp.int32)].add(route_part.astype(jnp.float32), mode='drop')
        return ((token_acc, route_acc), jnp.stack([grad_gate, grad_up, grad_down], 0))
    start = (jnp.zeros((TOKENS, D), jnp.float32), jnp.zeros((sentinel,), jnp.float32))
    (token_acc, route_acc), grads = lax.scan(per_expert, start, (weights, table))
    param_count = 3.0 * EXPERTS * D * HID
    root_mean = jnp.sqrt(jnp.sum(grads * grads) / param_count + 1e-06)
    clip_factor = jnp.minimum(1.0, 0.5 / root_mean)
    clipped = clip_factor * grads
    first_next = 0.9 * first_moment.astype(jnp.float32) + 0.1 * clipped
    second_next = 0.95 * second_moment.astype(jnp.float32) + 0.05 * clipped * clipped
    update = first_next / (1.0 - 0.9 ** ADAM_STEP) / (jnp.sqrt(second_next / (1.0 - 0.95 ** ADAM_STEP)) + 1e-08)
    token_grad = token_acc.astype(jnp.bfloat16)
    routing_grad = route_acc.reshape(TOKENS, TOPK).astype(jnp.bfloat16)
    return (token_grad, routing_grad, first_next.astype(jnp.bfloat16), second_next.astype(jnp.bfloat16), update.astype(jnp.bfloat16))
```

```python
import jax
import jax.numpy as jnp
from jax import lax
from jax.sharding import PartitionSpec as P

ADAM_STEP = 10


def on_device(tokens, cotangent, expert_ids, route_weights, weights, first_moment, second_moment):
    tok_count, model_width = tokens.shape
    topk_count = expert_ids.shape[1]
    local_experts = weights.shape[0]
    hidden_units = weights.shape[3]
    groups = lax.axis_size("ep")
    experts = local_experts * groups
    capacity = (tok_count * topk_count * 9 + 8 * experts - 1) // (8 * experts)
    pairs = tok_count * topk_count
    ids_flat = expert_ids.reshape(-1)
    onehot = (ids_flat[:, None] == jnp.arange(experts, dtype=jnp.int32)[None, :]).astype(jnp.int32)
    position = jnp.sum(jnp.cumsum(onehot, 0) * onehot, 1) - 1
    target = ids_flat * capacity + position
    token_row = jnp.arange(pairs, dtype=jnp.int32) // topk_count
    send_tokens = (
        jnp.zeros((experts * capacity, model_width), jnp.bfloat16).at[target].set(tokens[token_row])
    )
    send_cot = (
        jnp.zeros((experts * capacity, model_width), jnp.bfloat16)
        .at[target]
        .set(cotangent[token_row])
    )
    send_weight = (
        jnp.zeros((experts * capacity,), jnp.bfloat16).at[target].set(route_weights.reshape(-1))
    )
    send_tokens = send_tokens.reshape(experts, capacity, model_width)
    send_cot = send_cot.reshape(experts, capacity, model_width)
    send_weight = send_weight.reshape(experts, capacity)
    recv_x, recv_cot, recv_weight = (
        lax.all_to_all(send_tokens, "ep", split_axis=0, concat_axis=1, tiled=True),
        lax.all_to_all(send_cot, "ep", split_axis=0, concat_axis=1, tiled=True),
        lax.all_to_all(send_weight, "ep", split_axis=0, concat_axis=1, tiled=True),
    )
    w_gate = weights[:, 0]
    w_up = weights[:, 1]
    w_down = weights[:, 2]
    gate_val = jnp.einsum("erd,edh->erh", recv_x, w_gate, preferred_element_type=jnp.float32)
    up_val = jnp.einsum("erd,edh->erh", recv_x, w_up, preferred_element_type=jnp.float32)
    sigmoid_gate = jax.nn.sigmoid(gate_val)
    activated = gate_val * sigmoid_gate
    hidden = lax.optimization_barrier((activated * up_val).astype(jnp.bfloat16))
    back_val = jnp.einsum("erd,edh->erh", recv_cot, w_down, preferred_element_type=jnp.float32)
    route_part = lax.optimization_barrier(
        jnp.sum(hidden.astype(jnp.float32) * back_val, 2).astype(jnp.bfloat16)
    )
    row_weight = recv_weight.astype(jnp.float32)[:, :, None]
    scaled = row_weight * back_val
    dgate = (scaled * up_val * sigmoid_gate * (1.0 + gate_val * (1.0 - sigmoid_gate))).astype(
        jnp.bfloat16
    )
    dup = (scaled * activated).astype(jnp.bfloat16)
    down_cot = (row_weight * recv_cot.astype(jnp.float32)).astype(jnp.bfloat16)
    slot_back = jnp.einsum("erh,edh->erd", dgate, w_gate, preferred_element_type=jnp.float32)
    slot_back = slot_back + jnp.einsum(
        "erh,edh->erd", dup, w_up, preferred_element_type=jnp.float32
    )
    slot_back = lax.optimization_barrier(slot_back.astype(jnp.bfloat16))
    ret_rows, ret_route = (
        lax.all_to_all(slot_back, "ep", split_axis=1, concat_axis=0, tiled=True),
        lax.all_to_all(route_part, "ep", split_axis=1, concat_axis=0, tiled=True),
    )
    picked = ret_rows.reshape(experts * capacity, model_width)[target]
    token_grad = jnp.sum(
        picked.reshape(tok_count, topk_count, model_width).astype(jnp.float32), 1
    ).astype(jnp.bfloat16)
    routing_grad = ret_route.reshape(-1)[target].reshape(tok_count, topk_count)
    grad_local = jnp.stack(
        [
            jnp.einsum("erd,erh->edh", recv_x, dgate, preferred_element_type=jnp.float32),
            jnp.einsum("erd,erh->edh", recv_x, dup, preferred_element_type=jnp.float32),
            jnp.einsum("erd,erh->edh", down_cot, hidden, preferred_element_type=jnp.float32),
        ],
        1,
    )
    grad_share = lax.psum_scatter(grad_local, "dp", scatter_dimension=2, tiled=True)
    square_sum = lax.psum(jnp.sum(grad_share * grad_share), ("dp", "ep"))
    param_count = 3.0 * experts * model_width * hidden_units
    root_mean = jnp.sqrt(square_sum / param_count + 1e-06)
    clip_factor = jnp.minimum(1.0, 0.5 / root_mean)
    clipped = clip_factor * grad_share
    first_next = 0.9 * first_moment.astype(jnp.float32) + 0.1 * clipped
    second_next = 0.95 * second_moment.astype(jnp.float32) + 0.05 * clipped * clipped
    update = (
        first_next
        / (1.0 - 0.9**ADAM_STEP)
        / (jnp.sqrt(second_next / (1.0 - 0.95**ADAM_STEP)) + 1e-08)
    )
    return (
        token_grad,
        routing_grad,
        first_next.astype(jnp.bfloat16),
        second_next.astype(jnp.bfloat16),
        update.astype(jnp.bfloat16),
    )


def finish(grad_share, first_moment, second_moment, param_count):
    square_sum = lax.psum(jnp.sum(grad_share * grad_share), ("dp", "ep"))
    root_mean = jnp.sqrt(square_sum / param_count + 1e-06)
    clip_factor = jnp.minimum(1.0, 0.5 / root_mean)
    clipped = clip_factor * grad_share
    first_next = 0.9 * first_moment.astype(jnp.float32) + 0.1 * clipped
    second_next = 0.95 * second_moment.astype(jnp.float32) + 0.05 * clipped * clipped
    update = (
        first_next
        / (1.0 - 0.9**ADAM_STEP)
        / (jnp.sqrt(second_next / (1.0 - 0.95**ADAM_STEP)) + 1e-08)
    )
    return (
        first_next.astype(jnp.bfloat16),
        second_next.astype(jnp.bfloat16),
        update.astype(jnp.bfloat16),
    )


def on_device_gather(
    tokens, cotangent, expert_ids, route_weights, weights, first_moment, second_moment
):
    f32, bf16 = jnp.float32, jnp.bfloat16
    tok_count, model_width = tokens.shape
    topk_count = expert_ids.shape[1]
    hidden_units = weights.shape[3]
    groups = lax.axis_size("ep")
    experts = groups
    capacity = (tok_count * topk_count * 9 + 8 * experts - 1) // (8 * experts)
    rows = groups * capacity
    named = expert_ids[:, :, None] == jnp.arange(experts, dtype=jnp.int32)[None, None, :]
    table = jnp.sum(jnp.where(named, route_weights.astype(f32)[:, :, None], 0.0), 1).T.astype(bf16)
    mine = lax.all_to_all(table, "ep", split_axis=0, concat_axis=0, tiled=True)
    x_all = lax.all_gather(tokens, "ep")
    cot_all = lax.all_gather(cotangent, "ep")
    routed = mine > 0
    position = jnp.cumsum(routed.astype(jnp.int32), 1) - 1
    slots = jnp.arange(capacity, dtype=jnp.int32)
    pick = ((position[:, None, :] == slots[None, :, None]) & routed[:, None, :]).astype(bf16)
    recv_x = jnp.einsum("bst,btd->bsd", pick, x_all, preferred_element_type=f32).astype(bf16)
    recv_cot = jnp.einsum("bst,btd->bsd", pick, cot_all, preferred_element_type=f32).astype(bf16)
    recv_weight = jnp.sum(pick.astype(f32) * mine.astype(f32)[:, None, :], 2)
    recv_x = recv_x.reshape(rows, model_width)
    recv_cot = recv_cot.reshape(rows, model_width)
    row_weight = recv_weight.reshape(rows, 1)
    w_gate, w_up, w_down = weights[0, 0], weights[0, 1], weights[0, 2]
    gate_val = jnp.dot(recv_x, w_gate, preferred_element_type=f32)
    up_val = jnp.dot(recv_x, w_up, preferred_element_type=f32)
    sigmoid_gate = jax.nn.sigmoid(gate_val)
    activated = gate_val * sigmoid_gate
    hidden = lax.optimization_barrier((activated * up_val).astype(bf16))
    back_val = jnp.dot(recv_cot, w_down, preferred_element_type=f32)
    route_part = jnp.sum(hidden.astype(f32) * back_val, 1).astype(bf16)
    scaled = row_weight * back_val
    dgate = (scaled * up_val * sigmoid_gate * (1.0 + gate_val * (1.0 - sigmoid_gate))).astype(bf16)
    dup = (scaled * activated).astype(bf16)
    down_cot = (row_weight * recv_cot.astype(f32)).astype(bf16)
    by_row = (((0,), (0,)), ((), ()))
    grads = [
        lax.dot_general(recv_x, dgate, by_row, preferred_element_type=f32),
        lax.dot_general(recv_x, dup, by_row, preferred_element_type=f32),
        lax.dot_general(down_cot, hidden, by_row, preferred_element_type=f32),
    ]
    half = model_width // 2
    part = lax.axis_index("dp")
    kept = jnp.stack([lax.dynamic_slice_in_dim(g, part * half, half, 0) for g in grads])
    sent = jnp.stack([lax.dynamic_slice_in_dim(g, (1 - part) * half, half, 0) for g in grads])
    got = lax.ppermute(sent.astype(bf16), "dp", [(0, 1), (1, 0)])
    by_col = (((1,), (1,)), ((), ()))
    slot_back = lax.dot_general(dgate, w_gate, by_col, preferred_element_type=f32)
    slot_back = slot_back + lax.dot_general(dup, w_up, by_col, preferred_element_type=f32)
    slot_back = slot_back.astype(bf16).reshape(groups, capacity, model_width)
    spread = jnp.einsum("bst,bsd->btd", pick, slot_back, preferred_element_type=f32).astype(bf16)
    token_grad = lax.psum_scatter(spread, "ep", scatter_dimension=0)
    route_rows = jnp.sum(
        pick.astype(f32) * route_part.astype(f32).reshape(groups, capacity, 1), 1
    ).astype(bf16)
    route_back = lax.all_to_all(route_rows, "ep", split_axis=0, concat_axis=0, tiled=True)
    routing_grad = jnp.sum(
        jnp.where(named, route_back.T.astype(f32)[:, None, :], 0.0), 2
    ).astype(bf16)
    grad_share = (kept + got.astype(f32))[None]
    return (token_grad, routing_grad) + finish(
        grad_share, first_moment, second_moment, 3.0 * experts * model_width * hidden_units
    )


def fits(mesh):
    return mesh.shape["dp"] == 2 and mesh.shape["ep"] <= 16


def solution(mesh):
    in_specs = (
        P(("dp", "ep"), None),
        P(("dp", "ep"), None),
        P(("dp", "ep"), None),
        P(("dp", "ep"), None),
        P("ep", None, None, None),
        P("ep", None, "dp", None),
        P("ep", None, "dp", None),
    )
    out_specs = (
        P(("dp", "ep"), None),
        P(("dp", "ep"), None),
        P("ep", None, "dp", None),
        P("ep", None, "dp", None),
        P("ep", None, "dp", None),
    )
    return jax.shard_map(
        on_device_gather if fits(mesh) else on_device, mesh=mesh, in_specs=in_specs, out_specs=out_specs, check_vma=False
    )
```

```python
import functools

import jax
import jax.numpy as jnp
from jax import lax
from jax.experimental import pallas as pl
from jax.experimental.pallas import tpu as pltpu
from jax.sharding import PartitionSpec as P

ADAM_STEP = 10


def on_device(tokens, cotangent, expert_ids, route_weights, weights, first_moment, second_moment):
    tok_count, model_width = tokens.shape
    topk_count = expert_ids.shape[1]
    local_experts = weights.shape[0]
    hidden_units = weights.shape[3]
    groups = lax.axis_size("ep")
    experts = local_experts * groups
    capacity = (tok_count * topk_count * 9 + 8 * experts - 1) // (8 * experts)
    pairs = tok_count * topk_count
    ids_flat = expert_ids.reshape(-1)
    onehot = (ids_flat[:, None] == jnp.arange(experts, dtype=jnp.int32)[None, :]).astype(jnp.int32)
    position = jnp.sum(jnp.cumsum(onehot, 0) * onehot, 1) - 1
    target = ids_flat * capacity + position
    token_row = jnp.arange(pairs, dtype=jnp.int32) // topk_count
    send_tokens = (
        jnp.zeros((experts * capacity, model_width), jnp.bfloat16).at[target].set(tokens[token_row])
    )
    send_cot = (
        jnp.zeros((experts * capacity, model_width), jnp.bfloat16)
        .at[target]
        .set(cotangent[token_row])
    )
    send_weight = (
        jnp.zeros((experts * capacity,), jnp.bfloat16).at[target].set(route_weights.reshape(-1))
    )
    send_tokens = send_tokens.reshape(experts, capacity, model_width)
    send_cot = send_cot.reshape(experts, capacity, model_width)
    send_weight = send_weight.reshape(experts, capacity)
    recv_x, recv_cot, recv_weight = (
        lax.all_to_all(send_tokens, "ep", split_axis=0, concat_axis=1, tiled=True),
        lax.all_to_all(send_cot, "ep", split_axis=0, concat_axis=1, tiled=True),
        lax.all_to_all(send_weight, "ep", split_axis=0, concat_axis=1, tiled=True),
    )
    w_gate = weights[:, 0]
    w_up = weights[:, 1]
    w_down = weights[:, 2]
    gate_val = jnp.einsum("erd,edh->erh", recv_x, w_gate, preferred_element_type=jnp.float32)
    up_val = jnp.einsum("erd,edh->erh", recv_x, w_up, preferred_element_type=jnp.float32)
    sigmoid_gate = jax.nn.sigmoid(gate_val)
    activated = gate_val * sigmoid_gate
    hidden = lax.optimization_barrier((activated * up_val).astype(jnp.bfloat16))
    back_val = jnp.einsum("erd,edh->erh", recv_cot, w_down, preferred_element_type=jnp.float32)
    route_part = lax.optimization_barrier(
        jnp.sum(hidden.astype(jnp.float32) * back_val, 2).astype(jnp.bfloat16)
    )
    row_weight = recv_weight.astype(jnp.float32)[:, :, None]
    scaled = row_weight * back_val
    dgate = (scaled * up_val * sigmoid_gate * (1.0 + gate_val * (1.0 - sigmoid_gate))).astype(
        jnp.bfloat16
    )
    dup = (scaled * activated).astype(jnp.bfloat16)
    down_cot = (row_weight * recv_cot.astype(jnp.float32)).astype(jnp.bfloat16)
    slot_back = jnp.einsum("erh,edh->erd", dgate, w_gate, preferred_element_type=jnp.float32)
    slot_back = slot_back + jnp.einsum(
        "erh,edh->erd", dup, w_up, preferred_element_type=jnp.float32
    )
    slot_back = lax.optimization_barrier(slot_back.astype(jnp.bfloat16))
    ret_rows, ret_route = (
        lax.all_to_all(slot_back, "ep", split_axis=1, concat_axis=0, tiled=True),
        lax.all_to_all(route_part, "ep", split_axis=1, concat_axis=0, tiled=True),
    )
    picked = ret_rows.reshape(experts * capacity, model_width)[target]
    token_grad = jnp.sum(
        picked.reshape(tok_count, topk_count, model_width).astype(jnp.float32), 1
    ).astype(jnp.bfloat16)
    routing_grad = ret_route.reshape(-1)[target].reshape(tok_count, topk_count)
    grad_local = jnp.stack(
        [
            jnp.einsum("erd,erh->edh", recv_x, dgate, preferred_element_type=jnp.float32),
            jnp.einsum("erd,erh->edh", recv_x, dup, preferred_element_type=jnp.float32),
            jnp.einsum("erd,erh->edh", down_cot, hidden, preferred_element_type=jnp.float32),
        ],
        1,
    )
    grad_share = lax.psum_scatter(grad_local, "dp", scatter_dimension=2, tiled=True)
    square_sum = lax.psum(jnp.sum(grad_share * grad_share), ("dp", "ep"))
    param_count = 3.0 * experts * model_width * hidden_units
    root_mean = jnp.sqrt(square_sum / param_count + 1e-06)
    clip_factor = jnp.minimum(1.0, 0.5 / root_mean)
    clipped = clip_factor * grad_share
    first_next = 0.9 * first_moment.astype(jnp.float32) + 0.1 * clipped
    second_next = 0.95 * second_moment.astype(jnp.float32) + 0.05 * clipped * clipped
    update = (
        first_next
        / (1.0 - 0.9**ADAM_STEP)
        / (jnp.sqrt(second_next / (1.0 - 0.95**ADAM_STEP)) + 1e-08)
    )
    return (
        token_grad,
        routing_grad,
        first_next.astype(jnp.bfloat16),
        second_next.astype(jnp.bfloat16),
        update.astype(jnp.bfloat16),
    )


def finish(grad_share, first_moment, second_moment, param_count):
    square_sum = lax.psum(jnp.sum(grad_share * grad_share), ("dp", "ep"))
    root_mean = jnp.sqrt(square_sum / param_count + 1e-06)
    clip_factor = jnp.minimum(1.0, 0.5 / root_mean)
    clipped = clip_factor * grad_share
    first_next = 0.9 * first_moment.astype(jnp.float32) + 0.1 * clipped
    second_next = 0.95 * second_moment.astype(jnp.float32) + 0.05 * clipped * clipped
    update = (
        first_next
        / (1.0 - 0.9**ADAM_STEP)
        / (jnp.sqrt(second_next / (1.0 - 0.95**ADAM_STEP)) + 1e-08)
    )
    return (
        first_next.astype(jnp.bfloat16),
        second_next.astype(jnp.bfloat16),
        update.astype(jnp.bfloat16),
    )


MESH = pl.DeviceIdType.MESH
MIB = 1024 * 1024


def place(groups):
    me = lax.axis_index("ep")
    core = lax.rem(me, 2)
    side = lax.rem(me // 2, 2)
    return me // 4, side, core, groups // 4


def index_of(z, y, core):
    return (z * 2 + y) * 2 + core


def greet(z, y, core, depth, partner):
    barrier = pltpu.get_barrier_semaphore()

    def hello(device):
        pl.semaphore_signal(barrier, inc=1, device_id=device, device_id_type=MESH)

    hello({"ep": index_of(z, y, 1 - core)})
    hello({"ep": index_of(z, 1 - y, core)})
    expected = 2
    if partner is not None:
        hello(partner)
        expected = 3

    @pl.when(z > 0)
    def _():
        hello({"ep": index_of(z - 1, y, core)})

    @pl.when(z < depth - 1)
    def _():
        hello({"ep": index_of(z + 1, y, core)})

    pl.semaphore_wait(
        barrier, expected + jnp.where(z > 0, 1, 0) + jnp.where(z < depth - 1, 1, 0)
    )


def gather_kernel(groups, x_ref, c_ref, t_ref, xs, cs, ts, up_sem, down_sem, y_sem, core_sem, recv_sem, own_sem):
    z, y, core, depth = place(groups)
    me = index_of(z, y, core)
    arrays = ((x_ref, xs), (c_ref, cs), (t_ref, ts))
    greet(z, y, core, depth, None)

    def copies(block, source_own, sems, slot, device):
        return [
            pltpu.make_async_remote_copy(
                src_ref=own if source_own else full.at[block],
                dst_ref=full.at[block],
                send_sem=sems.at[i, slot],
                recv_sem=recv_sem.at[i, block],
                device_id={"ep": device},
                device_id_type=MESH,
            )
            for i, (own, full) in enumerate(arrays)
        ]

    def start(block, source_own, sems, slot, device):
        for copy in copies(block, source_own, sems, slot, device):
            copy.start()

    def arrived(block):
        for copy in copies(block, False, core_sem, 0, index_of(z, y, 1 - core)):
            copy.wait_recv()

    local = [
        pltpu.make_async_copy(own, full.at[me], own_sem.at[i])
        for i, (own, full) in enumerate(arrays)
    ]
    above, below = index_of(z + 1, y, core), index_of(z - 1, y, core)
    beside, sibling = index_of(z, 1 - y, core), index_of(z, y, 1 - core)

    @pl.when(z < depth - 1)
    def _():
        start(me, True, up_sem, z, above)

    @pl.when(z > 0)
    def _():
        start(me, True, down_sem, z, below)

    start(me, True, y_sem, z, beside)
    start(me, True, core_sem, z * 2 + y, sibling)
    for copy in local:
        copy.start()

    def pass_on(level, side):
        block = index_of(level, side, core)
        arrived(block)
        start(block, False, core_sem, level * 2 + side, sibling)
        return block

    for step in range(1, depth):
        @pl.when(z - step >= 0)
        def _():
            level = z - step
            block = index_of(level, y, core)
            arrived(block)

            @pl.when(z < depth - 1)
            def _():
                start(block, False, up_sem, level, above)

            start(block, False, y_sem, level, beside)
            start(block, False, core_sem, level * 2 + y, sibling)

        @pl.when(z + step <= depth - 1)
        def _():
            level = z + step
            block = index_of(level, y, core)
            arrived(block)

            @pl.when(z > 0)
            def _():
                start(block, False, down_sem, level, below)

            start(block, False, y_sem, level, beside)
            start(block, False, core_sem, level * 2 + y, sibling)

        if step == 1:
            pass_on(z, 1 - y)

        @pl.when(z - step >= 0)
        def _():
            pass_on(z - step, 1 - y)

        @pl.when(z + step <= depth - 1)
        def _():
            pass_on(z + step, 1 - y)

    for level in range(depth):
        for side in range(2):
            arrived(index_of(level, side, 1 - core))
    for copy in local:
        copy.wait()

    def sent(sems, slot, device):
        for copy in copies(me, True, sems, slot, device):
            copy.wait_send()

    for level in range(depth):
        @pl.when((z < depth - 1) & (level <= z))
        def _():
            sent(up_sem, level, above)

        @pl.when((z > 0) & (level >= z))
        def _():
            sent(down_sem, level, below)

        sent(y_sem, level, beside)
        for side in range(2):
            sent(core_sem, level * 2 + side, sibling)


def gather_blocks(tokens, cotangent, table, groups):
    depth = groups // 4
    any_space = pl.BlockSpec(memory_space=pl.ANY)
    dma = pltpu.SemaphoreType.DMA
    arrays = (tokens, cotangent, table)
    return pl.pallas_call(
        functools.partial(gather_kernel, groups),
        out_shape=[jax.ShapeDtypeStruct((groups,) + a.shape, a.dtype) for a in arrays],
        in_specs=[any_space] * 3,
        out_specs=[any_space] * 3,
        scratch_shapes=[
            dma((3, depth)),
            dma((3, depth)),
            dma((3, depth)),
            dma((3, 2 * depth)),
            dma((3, groups)),
            dma((3,)),
        ],
        compiler_params=pltpu.CompilerParams(
            collective_id=1, has_side_effects=True, vmem_limit_bytes=48 * MIB
        ),
    )(*arrays)


def combine_kernel(
    groups, sp, rt, g_ref, out, route_out, g_got,
    core_s, core_r, ys_s, ys_r, y_s, y_r, zs_s, zs_r, in_s, in_r,
    core_send, core_recv, y_send, y_recv, z_send, z_recv, g_sem,
):
    z, y, core, depth = place(groups)
    partner = {"dp": 1 - lax.axis_index("dp")}
    greet(z, y, core, depth, partner)
    g_copy = pltpu.make_async_remote_copy(
        src_ref=g_ref, dst_ref=g_got, send_sem=g_sem.at[0], recv_sem=g_sem.at[1],
        device_id=partner, device_id_type=MESH,
    )
    g_copy.start()
    chunk = 16
    chunks = sp.shape[1] // chunk
    f32, bf16 = jnp.float32, jnp.bfloat16

    def target(j):
        if j == depth - 1:
            return z
        low = jnp.where(depth - 1 - j > z, depth - 1 - j, depth - 2 - j)
        high = jnp.where(j < z, j, j + 1)
        return jnp.where(z < depth // 2, low, high)

    def pair(src, src_at, dst, dst_at, send, send_at, recv, recv_at, device):
        return [
            pltpu.make_async_remote_copy(
                src_ref=src[i].at[src_at], dst_ref=dst[i].at[dst_at],
                send_sem=send.at[i, send_at], recv_sem=recv.at[i, recv_at],
                device_id={"ep": device}, device_id_type=MESH,
            )
            for i in range(2)
        ]

    def core_copy(level, side):
        slot = level * 2 + side
        return pair(
            (sp, rt), index_of(level, side, 1 - core), (core_s, core_r), slot,
            core_send, slot, core_recv, slot, index_of(z, y, 1 - core),
        )

    def y_copy(level):
        return pair(
            (ys_s, ys_r), level, (y_s, y_r), level,
            y_send, level, y_recv, level, index_of(z, 1 - y, core),
        )

    def z_copy(level, going, slot):
        return pair(
            (zs_s, zs_r), level, (in_s, in_r), slot,
            z_send, level, z_recv, slot, index_of(going, y, core),
        )

    def add(result, terms):
        def body(i, carry):
            rows = pl.ds(pl.multiple_of(i * chunk, chunk), chunk)
            total = terms[0][0][terms[0][2], rows, :].astype(f32)
            for term in terms[1:]:
                total = total + term[0][term[2], rows, :].astype(f32)
            if result[2] is None:
                result[0][rows, :] = total.astype(bf16)
            else:
                result[0][result[2], rows, :] = total.astype(bf16)
            return carry

        lax.fori_loop(0, chunks, body, 0)
        small = terms[0][1][terms[0][2]].astype(f32)
        for term in terms[1:]:
            small = small + term[1][term[2]].astype(f32)
        if result[2] is None:
            result[1][...] = small.astype(bf16)
        else:
            result[1][result[2]] = small.astype(bf16)

    def each(copies, what):
        for copy in copies:
            getattr(copy, what)()

    for side in (1 - y, y):
        for j in range(depth):
            each(core_copy(target(j), side), "start")
    for j in range(depth):
        t = target(j)
        each(core_copy(t, 1 - y), "wait_recv")
        add((ys_s, ys_r, t), [(sp, rt, index_of(t, 1 - y, core)), (core_s, core_r, t * 2 + 1 - y)])
        each(y_copy(t), "start")
    for j in range(depth - 1):
        t = target(j)
        each(core_copy(t, y), "wait_recv")
        each(y_copy(t), "wait_recv")
        terms = [(sp, rt, index_of(t, y, core)), (core_s, core_r, t * 2 + y), (y_s, y_r, t)]
        upward = t > z
        slot = jnp.where(upward, t, depth + t)
        going = jnp.where(upward, z + 1, z - 1)
        more = (upward & (z > 0)) | (jnp.logical_not(upward) & (z < depth - 1))

        @pl.when(more)
        def _():
            each(z_copy(t, going, slot), "wait_recv")
            add((zs_s, zs_r, t), terms + [(in_s, in_r, slot)])

        @pl.when(jnp.logical_not(more))
        def _():
            add((zs_s, zs_r, t), terms)

        each(z_copy(t, going, slot), "start")
    each(core_copy(z, y), "wait_recv")
    each(y_copy(z), "wait_recv")
    terms = [(sp, rt, index_of(z, y, core)), (core_s, core_r, z * 2 + y), (y_s, y_r, z)]
    from_below, from_above = (in_s, in_r, z), (in_s, in_r, depth + z)
    beside = jnp.where(z > 0, z - 1, z + 1)

    @pl.when(z > 0)
    def _():
        each(z_copy(z, beside, z), "wait_recv")

    @pl.when(z < depth - 1)
    def _():
        each(z_copy(z, beside, depth + z), "wait_recv")

    @pl.when((z > 0) & (z < depth - 1))
    def _():
        add((out, route_out, None), terms + [from_below, from_above])

    @pl.when(z == 0)
    def _():
        add((out, route_out, None), terms + [from_above])

    @pl.when(z == depth - 1)
    def _():
        add((out, route_out, None), terms + [from_below])

    for j in range(depth):
        t = target(j)
        each(core_copy(t, 0), "wait_send")
        each(core_copy(t, 1), "wait_send")
        each(y_copy(t), "wait_send")
        if j < depth - 1:
            each(z_copy(t, beside, t), "wait_send")
    g_copy.wait()


def combine(spread, routes, sent, groups):
    depth = groups // 4
    bf16 = jnp.bfloat16
    big, small = spread.shape[1:], routes.shape[1:]
    vmem, any_space = pl.BlockSpec(memory_space=pltpu.VMEM), pl.BlockSpec(memory_space=pl.ANY)
    dma = pltpu.SemaphoreType.DMA

    def both(count):
        return [pltpu.VMEM((count,) + big, bf16), pltpu.VMEM((count,) + small, bf16)]

    return pl.pallas_call(
        functools.partial(combine_kernel, groups),
        out_shape=[
            jax.ShapeDtypeStruct(big, bf16),
            jax.ShapeDtypeStruct(small, bf16),
            jax.ShapeDtypeStruct(sent.shape, bf16),
        ],
        in_specs=[vmem, vmem, any_space],
        out_specs=[vmem, vmem, any_space],
        scratch_shapes=both(2 * depth) + both(depth) + both(depth) + both(depth) + both(2 * depth)
        + [
            dma((2, 2 * depth)), dma((2, 2 * depth)),
            dma((2, depth)), dma((2, depth)),
            dma((2, depth)), dma((2, 2 * depth)),
            dma((2,)),
        ],
        compiler_params=pltpu.CompilerParams(
            collective_id=2, has_side_effects=True, vmem_limit_bytes=48 * MIB
        ),
    )(spread, routes, sent)


def on_device_gather(
    tokens, cotangent, expert_ids, route_weights, weights, first_moment, second_moment
):
    f32, bf16 = jnp.float32, jnp.bfloat16
    tok_count, model_width = tokens.shape
    topk_count = expert_ids.shape[1]
    hidden_units = weights.shape[3]
    groups = lax.axis_size("ep")
    experts = groups
    capacity = (tok_count * topk_count * 9 + 8 * experts - 1) // (8 * experts)
    rows = groups * capacity
    named = expert_ids[:, :, None] == jnp.arange(experts, dtype=jnp.int32)[None, None, :]
    table = jnp.sum(jnp.where(named, route_weights.astype(f32)[:, :, None], 0.0), 1).T.astype(bf16)
    x_all, cot_all, tables = gather_blocks(tokens, cotangent, table, groups)
    me = lax.axis_index("ep")
    mine = lax.dynamic_slice_in_dim(tables, me, 1, 1)[:, 0, :]
    routed = mine > 0
    position = jnp.cumsum(routed.astype(jnp.int32), 1) - 1
    slots = jnp.arange(capacity, dtype=jnp.int32)
    pick = ((position[:, None, :] == slots[None, :, None]) & routed[:, None, :]).astype(bf16)
    recv_x = jnp.einsum("bst,btd->bsd", pick, x_all, preferred_element_type=f32).astype(bf16)
    recv_cot = jnp.einsum("bst,btd->bsd", pick, cot_all, preferred_element_type=f32).astype(bf16)
    recv_weight = jnp.sum(pick.astype(f32) * mine.astype(f32)[:, None, :], 2)
    recv_x = recv_x.reshape(rows, model_width)
    recv_cot = recv_cot.reshape(rows, model_width)
    row_weight = recv_weight.reshape(rows, 1)
    w_gate, w_up, w_down = weights[0, 0], weights[0, 1], weights[0, 2]
    gate_val = jnp.dot(recv_x, w_gate, preferred_element_type=f32)
    up_val = jnp.dot(recv_x, w_up, preferred_element_type=f32)
    sigmoid_gate = jax.nn.sigmoid(gate_val)
    activated = gate_val * sigmoid_gate
    hidden = lax.optimization_barrier((activated * up_val).astype(bf16))
    back_val = jnp.dot(recv_cot, w_down, preferred_element_type=f32)
    route_part = jnp.sum(hidden.astype(f32) * back_val, 1).astype(bf16)
    scaled = row_weight * back_val
    dgate = (scaled * up_val * sigmoid_gate * (1.0 + gate_val * (1.0 - sigmoid_gate))).astype(bf16)
    dup = (scaled * activated).astype(bf16)
    down_cot = (row_weight * recv_cot.astype(f32)).astype(bf16)
    by_row = (((0,), (0,)), ((), ()))
    grads = [
        lax.dot_general(recv_x, dgate, by_row, preferred_element_type=f32),
        lax.dot_general(recv_x, dup, by_row, preferred_element_type=f32),
        lax.dot_general(down_cot, hidden, by_row, preferred_element_type=f32),
    ]
    half = model_width // 2
    part = lax.axis_index("dp")
    kept = jnp.stack([lax.dynamic_slice_in_dim(g, part * half, half, 0) for g in grads])
    sent = jnp.stack([lax.dynamic_slice_in_dim(g, (1 - part) * half, half, 0) for g in grads])
    by_col = (((1,), (1,)), ((), ()))
    slot_back = lax.dot_general(dgate, w_gate, by_col, preferred_element_type=f32)
    slot_back = slot_back + lax.dot_general(dup, w_up, by_col, preferred_element_type=f32)
    slot_back = slot_back.astype(bf16).reshape(groups, capacity, model_width)
    spread = jnp.einsum("bst,bsd->btd", pick, slot_back, preferred_element_type=f32).astype(bf16)
    route_rows = jnp.sum(
        pick.astype(f32) * route_part.astype(f32).reshape(groups, capacity, 1), 1
    )
    my_row = jnp.arange(experts, dtype=jnp.int32)[None, :, None] == me
    routes = jnp.where(my_row, route_rows[:, None, :], 0.0).astype(bf16)
    token_grad, route_back, got = combine(spread, routes, sent.astype(bf16), groups)
    routing_grad = jnp.sum(
        jnp.where(named, route_back.T.astype(f32)[:, None, :], 0.0), 2
    ).astype(bf16)
    grad_share = (kept + got.astype(f32))[None]
    return (token_grad, routing_grad) + finish(
        grad_share, first_moment, second_moment, 3.0 * experts * model_width * hidden_units
    )


def fits(mesh):
    return mesh.shape["dp"] == 2 and mesh.shape["ep"] == 16


def solution(mesh):
    in_specs = (
        P(("dp", "ep"), None),
        P(("dp", "ep"), None),
        P(("dp", "ep"), None),
        P(("dp", "ep"), None),
        P("ep", None, None, None),
        P("ep", None, "dp", None),
        P("ep", None, "dp", None),
    )
    out_specs = (
        P(("dp", "ep"), None),
        P(("dp", "ep"), None),
        P("ep", None, "dp", None),
        P("ep", None, "dp", None),
        P("ep", None, "dp", None),
    )
    return jax.shard_map(
        on_device_gather if fits(mesh) else on_device, mesh=mesh, in_specs=in_specs, out_specs=out_specs, check_vma=False
    )
```

```python
import functools

import jax
import jax.numpy as jnp
from jax import lax
from jax.experimental import pallas as pl
from jax.experimental.pallas import tpu as pltpu
from jax.sharding import PartitionSpec as P

ADAM_STEP = 10


def on_device(tokens, cotangent, expert_ids, route_weights, weights, first_moment, second_moment):
    tok_count, model_width = tokens.shape
    topk_count = expert_ids.shape[1]
    local_experts = weights.shape[0]
    hidden_units = weights.shape[3]
    groups = lax.axis_size("ep")
    experts = local_experts * groups
    capacity = (tok_count * topk_count * 9 + 8 * experts - 1) // (8 * experts)
    pairs = tok_count * topk_count
    ids_flat = expert_ids.reshape(-1)
    onehot = (ids_flat[:, None] == jnp.arange(experts, dtype=jnp.int32)[None, :]).astype(jnp.int32)
    position = jnp.sum(jnp.cumsum(onehot, 0) * onehot, 1) - 1
    target = ids_flat * capacity + position
    token_row = jnp.arange(pairs, dtype=jnp.int32) // topk_count
    send_tokens = (
        jnp.zeros((experts * capacity, model_width), jnp.bfloat16).at[target].set(tokens[token_row])
    )
    send_cot = (
        jnp.zeros((experts * capacity, model_width), jnp.bfloat16)
        .at[target]
        .set(cotangent[token_row])
    )
    send_weight = (
        jnp.zeros((experts * capacity,), jnp.bfloat16).at[target].set(route_weights.reshape(-1))
    )
    send_tokens = send_tokens.reshape(experts, capacity, model_width)
    send_cot = send_cot.reshape(experts, capacity, model_width)
    send_weight = send_weight.reshape(experts, capacity)
    recv_x, recv_cot, recv_weight = (
        lax.all_to_all(send_tokens, "ep", split_axis=0, concat_axis=1, tiled=True),
        lax.all_to_all(send_cot, "ep", split_axis=0, concat_axis=1, tiled=True),
        lax.all_to_all(send_weight, "ep", split_axis=0, concat_axis=1, tiled=True),
    )
    w_gate = weights[:, 0]
    w_up = weights[:, 1]
    w_down = weights[:, 2]
    gate_val = jnp.einsum("erd,edh->erh", recv_x, w_gate, preferred_element_type=jnp.float32)
    up_val = jnp.einsum("erd,edh->erh", recv_x, w_up, preferred_element_type=jnp.float32)
    sigmoid_gate = jax.nn.sigmoid(gate_val)
    activated = gate_val * sigmoid_gate
    hidden = lax.optimization_barrier((activated * up_val).astype(jnp.bfloat16))
    back_val = jnp.einsum("erd,edh->erh", recv_cot, w_down, preferred_element_type=jnp.float32)
    route_part = lax.optimization_barrier(
        jnp.sum(hidden.astype(jnp.float32) * back_val, 2).astype(jnp.bfloat16)
    )
    row_weight = recv_weight.astype(jnp.float32)[:, :, None]
    scaled = row_weight * back_val
    dgate = (scaled * up_val * sigmoid_gate * (1.0 + gate_val * (1.0 - sigmoid_gate))).astype(
        jnp.bfloat16
    )
    dup = (scaled * activated).astype(jnp.bfloat16)
    down_cot = (row_weight * recv_cot.astype(jnp.float32)).astype(jnp.bfloat16)
    slot_back = jnp.einsum("erh,edh->erd", dgate, w_gate, preferred_element_type=jnp.float32)
    slot_back = slot_back + jnp.einsum(
        "erh,edh->erd", dup, w_up, preferred_element_type=jnp.float32
    )
    slot_back = lax.optimization_barrier(slot_back.astype(jnp.bfloat16))
    ret_rows, ret_route = (
        lax.all_to_all(slot_back, "ep", split_axis=1, concat_axis=0, tiled=True),
        lax.all_to_all(route_part, "ep", split_axis=1, concat_axis=0, tiled=True),
    )
    picked = ret_rows.reshape(experts * capacity, model_width)[target]
    token_grad = jnp.sum(
        picked.reshape(tok_count, topk_count, model_width).astype(jnp.float32), 1
    ).astype(jnp.bfloat16)
    routing_grad = ret_route.reshape(-1)[target].reshape(tok_count, topk_count)
    grad_local = jnp.stack(
        [
            jnp.einsum("erd,erh->edh", recv_x, dgate, preferred_element_type=jnp.float32),
            jnp.einsum("erd,erh->edh", recv_x, dup, preferred_element_type=jnp.float32),
            jnp.einsum("erd,erh->edh", down_cot, hidden, preferred_element_type=jnp.float32),
        ],
        1,
    )
    grad_share = lax.psum_scatter(grad_local, "dp", scatter_dimension=2, tiled=True)
    square_sum = lax.psum(jnp.sum(grad_share * grad_share), ("dp", "ep"))
    param_count = 3.0 * experts * model_width * hidden_units
    root_mean = jnp.sqrt(square_sum / param_count + 1e-06)
    clip_factor = jnp.minimum(1.0, 0.5 / root_mean)
    clipped = clip_factor * grad_share
    first_next = 0.9 * first_moment.astype(jnp.float32) + 0.1 * clipped
    second_next = 0.95 * second_moment.astype(jnp.float32) + 0.05 * clipped * clipped
    update = (
        first_next
        / (1.0 - 0.9**ADAM_STEP)
        / (jnp.sqrt(second_next / (1.0 - 0.95**ADAM_STEP)) + 1e-08)
    )
    return (
        token_grad,
        routing_grad,
        first_next.astype(jnp.bfloat16),
        second_next.astype(jnp.bfloat16),
        update.astype(jnp.bfloat16),
    )


def finish(grad_share, square_sum, first_moment, second_moment, param_count):
    root_mean = jnp.sqrt(square_sum / param_count + 1e-06)
    clip_factor = jnp.minimum(1.0, 0.5 / root_mean)
    clipped = clip_factor * grad_share
    first_next = 0.9 * first_moment.astype(jnp.float32) + 0.1 * clipped
    second_next = 0.95 * second_moment.astype(jnp.float32) + 0.05 * clipped * clipped
    update = (
        first_next
        / (1.0 - 0.9**ADAM_STEP)
        / (jnp.sqrt(second_next / (1.0 - 0.95**ADAM_STEP)) + 1e-08)
    )
    return (
        first_next.astype(jnp.bfloat16),
        second_next.astype(jnp.bfloat16),
        update.astype(jnp.bfloat16),
    )


MESH = pl.DeviceIdType.MESH
MIB = 1024 * 1024


def place(groups):
    me = lax.axis_index("ep")
    core = lax.rem(me, 2)
    side = lax.rem(me // 2, 2)
    return me // 4, side, core, groups // 4


def index_of(z, y, core):
    return (z * 2 + y) * 2 + core


def greet(z, y, core, depth, partner):
    barrier = pltpu.get_barrier_semaphore()

    def hello(device):
        pl.semaphore_signal(barrier, inc=1, device_id=device, device_id_type=MESH)

    hello({"ep": index_of(z, y, 1 - core)})
    hello({"ep": index_of(z, 1 - y, core)})
    expected = 2
    if partner is not None:
        hello(partner)
        expected = 3

    for level in range(depth):
        @pl.when(z != level)
        def _():
            hello({"ep": index_of(level, y, core)})

    pl.semaphore_wait(barrier, expected + depth - 1)


def gather_kernel(groups, x_ref, c_ref, t_ref, xs, cs, ts, up_sem, down_sem, y_sem, core_sem, recv_sem, own_sem):
    z, y, core, depth = place(groups)
    me = index_of(z, y, core)
    arrays = ((x_ref, xs), (c_ref, cs), (t_ref, ts))
    greet(z, y, core, depth, None)

    above, below = index_of(z + 1, y, core), index_of(z - 1, y, core)
    beside, sibling = index_of(z, 1 - y, core), index_of(z, y, 1 - core)
    paired = z + 1 - 2 * lax.rem(z, 2)

    def copy(i, block, source_own, sems, slot, device):
        own, full = arrays[i]
        return pltpu.make_async_remote_copy(
            src_ref=own if source_own else full.at[block],
            dst_ref=full.at[block],
            send_sem=sems.at[i, slot],
            recv_sem=recv_sem.at[i, block],
            device_id={"ep": device},
            device_id_type=MESH,
        )

    def arrived(i, block):
        copy(i, block, False, core_sem, 0, sibling).wait_recv()

    local = [
        pltpu.make_async_copy(own, full.at[me], own_sem.at[i])
        for i, (own, full) in enumerate(arrays)
    ]
    for i in range(3):
        @pl.when(z < depth - 1)
        def _():
            copy(i, me, True, up_sem, z, above).start()

        @pl.when(z > 0)
        def _():
            copy(i, me, True, down_sem, z, below).start()

        copy(i, me, True, y_sem, z, beside).start()
        copy(i, me, True, core_sem, z * 2 + y, sibling).start()
    for each in local:
        each.start()

    def spread_column(i, level, onward, sems, device):
        block = index_of(level, y, core)
        arrived(i, block)

        @pl.when(onward)
        def _():
            copy(i, block, False, sems, level, device).start()

        if i == 1:
            @pl.when(level != paired)
            def _():
                copy(i, block, False, y_sem, level, beside).start()
        else:
            copy(i, block, False, y_sem, level, beside).start()
        copy(i, block, False, core_sem, level * 2 + y, sibling).start()

    for step in range(1, depth):
        for i in range(3):
            @pl.when(z - step >= 0)
            def _():
                spread_column(i, z - step, z < depth - 1, up_sem, above)

            @pl.when(z + step <= depth - 1)
            def _():
                spread_column(i, z + step, z > 0, down_sem, below)

        if step == 1:
            far = index_of(z, 1 - y, core)
            for i in range(3):
                arrived(i, far)
                if i == 1:
                    copy(i, far, False, y_sem, paired, index_of(paired, y, core)).start()
                copy(i, far, False, core_sem, z * 2 + 1 - y, sibling).start()

    def pass_on(level):
        far = index_of(level, 1 - y, core)
        for i in range(3):
            arrived(i, far)
            copy(i, far, False, core_sem, level * 2 + 1 - y, sibling).start()

    for step in range(1, depth):
        @pl.when(z - step >= 0)
        def _():
            pass_on(z - step)

        @pl.when(z + step <= depth - 1)
        def _():
            pass_on(z + step)

    for level in range(depth):
        for side in range(2):
            for i in range(3):
                arrived(i, index_of(level, side, 1 - core))
    for each in local:
        each.wait()

    def sent(sems, slot, device):
        for i in range(3):
            copy(i, me, True, sems, slot, device).wait_send()

    for level in range(depth):
        @pl.when((z < depth - 1) & (level <= z))
        def _():
            sent(up_sem, level, above)

        @pl.when((z > 0) & (level >= z))
        def _():
            sent(down_sem, level, below)

        sent(y_sem, level, beside)
        for side in range(2):
            sent(core_sem, level * 2 + side, sibling)


def gather_blocks(tokens, cotangent, table, groups):
    depth = groups // 4
    any_space = pl.BlockSpec(memory_space=pl.ANY)
    dma = pltpu.SemaphoreType.DMA
    arrays = (tokens, cotangent, table)
    return pl.pallas_call(
        functools.partial(gather_kernel, groups),
        out_shape=[jax.ShapeDtypeStruct((groups,) + a.shape, a.dtype) for a in arrays],
        in_specs=[any_space] * 3,
        out_specs=[any_space] * 3,
        scratch_shapes=[
            dma((3, depth)),
            dma((3, depth)),
            dma((3, depth)),
            dma((3, 2 * depth)),
            dma((3, groups)),
            dma((3,)),
        ],
        compiler_params=pltpu.CompilerParams(
            collective_id=1, has_side_effects=True, vmem_limit_bytes=48 * MIB
        ),
    )(*arrays)


def combine_kernel(
    groups, sp, rt, g_ref, kept, out, route_out, g_got, squares,
    core_s, core_r, ys_s, ys_r, y_s, y_r, zs_s, zs_r, in_s, in_r,
    core_send, core_recv, y_send, y_recv, z_send, z_recv, g_sem, n_out, n_in, n_send, n_recv,
):
    z, y, core, depth = place(groups)
    partner = {"dp": 1 - lax.axis_index("dp")}
    greet(z, y, core, depth, partner)
    g_copy = pltpu.make_async_remote_copy(
        src_ref=g_ref, dst_ref=g_got, send_sem=g_sem.at[0], recv_sem=g_sem.at[1],
        device_id=partner, device_id_type=MESH,
    )
    g_copy.start()
    chunk = 16
    chunks = sp.shape[1] // chunk
    f32, bf16 = jnp.float32, jnp.bfloat16

    def target(j):
        if j == depth - 1:
            return z
        low = jnp.where(depth - 1 - j > z, depth - 1 - j, depth - 2 - j)
        high = jnp.where(j < z, j, j + 1)
        return jnp.where(z < depth // 2, low, high)

    def pair(src, src_at, dst, dst_at, send, send_at, recv, recv_at, device):
        return [
            pltpu.make_async_remote_copy(
                src_ref=src[i].at[src_at], dst_ref=dst[i].at[dst_at],
                send_sem=send.at[i, send_at], recv_sem=recv.at[i, recv_at],
                device_id={"ep": device}, device_id_type=MESH,
            )
            for i in range(2)
        ]

    def core_copy(level, side):
        slot = level * 2 + side
        return pair(
            (sp, rt), index_of(level, side, 1 - core), (core_s, core_r), slot,
            core_send, slot, core_recv, slot, index_of(z, y, 1 - core),
        )

    def y_copy(level):
        return pair(
            (ys_s, ys_r), level, (y_s, y_r), level,
            y_send, level, y_recv, level, index_of(z, 1 - y, core),
        )

    def z_copy(level, going, slot):
        return pair(
            (zs_s, zs_r), level, (in_s, in_r), slot,
            z_send, level, z_recv, slot, index_of(going, y, core),
        )

    def add(result, terms):
        def body(i, carry):
            rows = pl.ds(pl.multiple_of(i * chunk, chunk), chunk)
            total = terms[0][0][terms[0][2], rows, :].astype(f32)
            for term in terms[1:]:
                total = total + term[0][term[2], rows, :].astype(f32)
            if result[2] is None:
                result[0][rows, :] = total.astype(bf16)
            else:
                result[0][result[2], rows, :] = total.astype(bf16)
            return carry

        lax.fori_loop(0, chunks, body, 0)
        small = terms[0][1][terms[0][2]].astype(f32)
        for term in terms[1:]:
            small = small + term[1][term[2]].astype(f32)
        if result[2] is None:
            result[1][...] = small.astype(bf16)
        else:
            result[1][result[2]] = small.astype(bf16)

    def each(copies, what):
        for copy in copies:
            getattr(copy, what)()

    for side in (1 - y, y):
        for j in range(depth):
            each(core_copy(target(j), side), "start")
    for j in range(depth):
        t = target(j)
        each(core_copy(t, 1 - y), "wait_recv")
        add((ys_s, ys_r, t), [(sp, rt, index_of(t, 1 - y, core)), (core_s, core_r, t * 2 + 1 - y)])
        each(y_copy(t), "start")
    for j in range(depth - 1):
        t = target(j)
        each(core_copy(t, y), "wait_recv")
        each(y_copy(t), "wait_recv")
        terms = [(sp, rt, index_of(t, y, core)), (core_s, core_r, t * 2 + y), (y_s, y_r, t)]
        upward = t > z
        slot = jnp.where(upward, t, depth + t)
        going = jnp.where(upward, z + 1, z - 1)
        more = (upward & (z > 0)) | (jnp.logical_not(upward) & (z < depth - 1))

        @pl.when(more)
        def _():
            each(z_copy(t, going, slot), "wait_recv")
            add((zs_s, zs_r, t), terms + [(in_s, in_r, slot)])

        @pl.when(jnp.logical_not(more))
        def _():
            add((zs_s, zs_r, t), terms)

        each(z_copy(t, going, slot), "start")
    each(core_copy(z, y), "wait_recv")
    each(y_copy(z), "wait_recv")
    terms = [(sp, rt, index_of(z, y, core)), (core_s, core_r, z * 2 + y), (y_s, y_r, z)]
    from_below, from_above = (in_s, in_r, z), (in_s, in_r, depth + z)
    beside = jnp.where(z > 0, z - 1, z + 1)

    @pl.when(z > 0)
    def _():
        each(z_copy(z, beside, z), "wait_recv")

    @pl.when(z < depth - 1)
    def _():
        each(z_copy(z, beside, depth + z), "wait_recv")

    @pl.when((z > 0) & (z < depth - 1))
    def _():
        add((out, route_out, None), terms + [from_below, from_above])

    @pl.when(z == 0)
    def _():
        add((out, route_out, None), terms + [from_above])

    @pl.when(z == depth - 1)
    def _():
        add((out, route_out, None), terms + [from_below])

    for j in range(depth):
        t = target(j)
        each(core_copy(t, 0), "wait_send")
        each(core_copy(t, 1), "wait_send")
        each(y_copy(t), "wait_send")
        if j < depth - 1:
            each(z_copy(t, beside, t), "wait_send")
    g_copy.wait()

    units, width, piece = kept.shape[0], kept.shape[2], 32

    def square(i, carry):
        rows = pl.ds(pl.multiple_of(i * piece, piece), piece)
        for unit in range(units):
            share = kept[unit, rows, :] + g_got[unit, rows, :].astype(f32)
            carry = carry + share * share
        return carry

    sums = lax.fori_loop(0, kept.shape[1] // piece, square, jnp.zeros((piece, width), f32))
    sums = sum(sums[i * 8:(i + 1) * 8] for i in range(piece // 8))
    sums = sum(sums[:, i * 128:(i + 1) * 128] for i in range(width // 128))

    def share_sum(src, dst, device, recv):
        return pltpu.make_async_remote_copy(
            src_ref=n_out.at[src], dst_ref=n_in.at[dst], send_sem=n_send.at[recv],
            recv_sem=n_recv.at[dst], device_id=device, device_id_type=MESH,
        )

    for stage, device in enumerate(
        (partner, {"ep": index_of(z, y, 1 - core)}, {"ep": index_of(z, 1 - y, core)})
    ):
        n_out[stage] = sums
        trade = share_sum(stage, stage, device, stage)
        trade.start()
        trade.wait()
        sums = sums + n_in[stage]
    n_out[3] = sums
    for level in range(depth):
        @pl.when(z != level)
        def _():
            share_sum(3, 3 + z, {"ep": index_of(level, y, core)}, 3 + level).start()

    squares[...] = sums
    for level in range(depth):
        @pl.when(z != level)
        def _():
            share_sum(3, 3 + level, {"ep": index_of(level, y, core)}, 3 + level).wait()
            squares[...] += n_in[3 + level]


def combine(spread, routes, sent, kept, groups):
    depth = groups // 4
    bf16 = jnp.bfloat16
    big, small = spread.shape[1:], routes.shape[1:]
    vmem, any_space = pl.BlockSpec(memory_space=pltpu.VMEM), pl.BlockSpec(memory_space=pl.ANY)
    dma = pltpu.SemaphoreType.DMA

    def both(count):
        return [pltpu.VMEM((count,) + big, bf16), pltpu.VMEM((count,) + small, bf16)]

    return pl.pallas_call(
        functools.partial(combine_kernel, groups),
        out_shape=[
            jax.ShapeDtypeStruct(big, bf16),
            jax.ShapeDtypeStruct(small, bf16),
            jax.ShapeDtypeStruct(sent.shape, bf16),
            jax.ShapeDtypeStruct((8, 128), jnp.float32),
        ],
        in_specs=[vmem, vmem, any_space, vmem],
        out_specs=[vmem, vmem, vmem, vmem],
        scratch_shapes=both(2 * depth) + both(depth) + both(depth) + both(depth) + both(2 * depth)
        + [
            dma((2, 2 * depth)), dma((2, 2 * depth)),
            dma((2, depth)), dma((2, depth)),
            dma((2, depth)), dma((2, 2 * depth)),
            dma((2,)),
            pltpu.VMEM((4, 8, 128), jnp.float32),
            pltpu.VMEM((3 + depth, 8, 128), jnp.float32),
            dma((3 + depth,)),
            dma((3 + depth,)),
        ],
        compiler_params=pltpu.CompilerParams(
            collective_id=2, has_side_effects=True, vmem_limit_bytes=52 * MIB
        ),
    )(spread, routes, sent, kept)


def on_device_gather(
    tokens, cotangent, expert_ids, route_weights, weights, first_moment, second_moment
):
    f32, bf16 = jnp.float32, jnp.bfloat16
    tok_count, model_width = tokens.shape
    topk_count = expert_ids.shape[1]
    hidden_units = weights.shape[3]
    groups = lax.axis_size("ep")
    experts = groups
    capacity = (tok_count * topk_count * 9 + 8 * experts - 1) // (8 * experts)
    rows = groups * capacity
    named = expert_ids[:, :, None] == jnp.arange(experts, dtype=jnp.int32)[None, None, :]
    table = jnp.sum(jnp.where(named, route_weights.astype(f32)[:, :, None], 0.0), 1).T.astype(bf16)
    x_all, cot_all, tables = gather_blocks(tokens, cotangent, table, groups)
    me = lax.axis_index("ep")
    mine = lax.dynamic_slice_in_dim(tables, me, 1, 1)[:, 0, :]
    routed = mine > 0
    position = jnp.cumsum(routed.astype(jnp.int32), 1) - 1
    slots = jnp.arange(capacity, dtype=jnp.int32)
    pick = ((position[:, None, :] == slots[None, :, None]) & routed[:, None, :]).astype(bf16)
    recv_x = jnp.einsum("bst,btd->bsd", pick, x_all, preferred_element_type=f32).astype(bf16)
    recv_cot = jnp.einsum("bst,btd->bsd", pick, cot_all, preferred_element_type=f32).astype(bf16)
    recv_weight = jnp.sum(pick.astype(f32) * mine.astype(f32)[:, None, :], 2)
    recv_x = recv_x.reshape(rows, model_width)
    recv_cot = recv_cot.reshape(rows, model_width)
    row_weight = recv_weight.reshape(rows, 1)
    w_gate, w_up, w_down = weights[0, 0], weights[0, 1], weights[0, 2]
    gate_val = jnp.dot(recv_x, w_gate, preferred_element_type=f32)
    up_val = jnp.dot(recv_x, w_up, preferred_element_type=f32)
    sigmoid_gate = jax.nn.sigmoid(gate_val)
    activated = gate_val * sigmoid_gate
    hidden = lax.optimization_barrier((activated * up_val).astype(bf16))
    back_val = jnp.dot(recv_cot, w_down, preferred_element_type=f32)
    route_part = jnp.sum(hidden.astype(f32) * back_val, 1).astype(bf16)
    scaled = row_weight * back_val
    dgate = (scaled * up_val * sigmoid_gate * (1.0 + gate_val * (1.0 - sigmoid_gate))).astype(bf16)
    dup = (scaled * activated).astype(bf16)
    down_cot = (row_weight * recv_cot.astype(f32)).astype(bf16)
    by_row = (((0,), (0,)), ((), ()))
    half = model_width // 2
    part = lax.axis_index("dp")

    def grads(owner, kind):
        columns = lambda a: lax.dynamic_slice_in_dim(a, owner * half, half, 1)
        return jnp.stack(
            [
                lax.dot_general(columns(rows_of), by, by_row, preferred_element_type=f32).astype(kind)
                for rows_of, by in ((recv_x, dgate), (recv_x, dup), (down_cot, hidden))
            ]
        )

    sent, kept = grads(1 - part, bf16), grads(part, f32)
    by_col = (((1,), (1,)), ((), ()))
    slot_back = lax.dot_general(dgate, w_gate, by_col, preferred_element_type=f32)
    slot_back = slot_back + lax.dot_general(dup, w_up, by_col, preferred_element_type=f32)
    slot_back = slot_back.astype(bf16).reshape(groups, capacity, model_width)
    spread = jnp.einsum("bst,bsd->btd", pick, slot_back, preferred_element_type=f32).astype(bf16)
    route_rows = jnp.sum(
        pick.astype(f32) * route_part.astype(f32).reshape(groups, capacity, 1), 1
    )
    my_row = jnp.arange(experts, dtype=jnp.int32)[None, :, None] == me
    routes = jnp.where(my_row, route_rows[:, None, :], 0.0).astype(bf16)
    token_grad, route_back, got, squares = combine(spread, routes, sent, kept, groups)
    routing_grad = jnp.sum(
        jnp.where(named, route_back.T.astype(f32)[:, None, :], 0.0), 2
    ).astype(bf16)
    grad_share = (kept + got.astype(f32))[None]
    return (token_grad, routing_grad) + finish(
        grad_share,
        jnp.sum(squares),
        first_moment,
        second_moment,
        3.0 * experts * model_width * hidden_units,
    )


def fits(mesh):
    return mesh.shape["dp"] == 2 and mesh.shape["ep"] == 16


def solution(mesh):
    in_specs = (
        P(("dp", "ep"), None),
        P(("dp", "ep"), None),
        P(("dp", "ep"), None),
        P(("dp", "ep"), None),
        P("ep", None, None, None),
        P("ep", None, "dp", None),
        P("ep", None, "dp", None),
    )
    out_specs = (
        P(("dp", "ep"), None),
        P(("dp", "ep"), None),
        P("ep", None, "dp", None),
        P("ep", None, "dp", None),
        P("ep", None, "dp", None),
    )
    return jax.shard_map(
        on_device_gather if fits(mesh) else on_device, mesh=mesh, in_specs=in_specs, out_specs=out_specs, check_vma=False
    )
```

```python
import functools

import jax
import jax.numpy as jnp
from jax import lax
from jax.experimental import pallas as pl
from jax.experimental.pallas import tpu as pltpu
from jax.sharding import PartitionSpec as P

ADAM_STEP = 10


def on_device(tokens, cotangent, expert_ids, route_weights, weights, first_moment, second_moment):
    tok_count, model_width = tokens.shape
    topk_count = expert_ids.shape[1]
    local_experts = weights.shape[0]
    hidden_units = weights.shape[3]
    groups = lax.axis_size("ep")
    experts = local_experts * groups
    capacity = (tok_count * topk_count * 9 + 8 * experts - 1) // (8 * experts)
    pairs = tok_count * topk_count
    ids_flat = expert_ids.reshape(-1)
    onehot = (ids_flat[:, None] == jnp.arange(experts, dtype=jnp.int32)[None, :]).astype(jnp.int32)
    position = jnp.sum(jnp.cumsum(onehot, 0) * onehot, 1) - 1
    target = ids_flat * capacity + position
    token_row = jnp.arange(pairs, dtype=jnp.int32) // topk_count
    send_tokens = (
        jnp.zeros((experts * capacity, model_width), jnp.bfloat16).at[target].set(tokens[token_row])
    )
    send_cot = (
        jnp.zeros((experts * capacity, model_width), jnp.bfloat16)
        .at[target]
        .set(cotangent[token_row])
    )
    send_weight = (
        jnp.zeros((experts * capacity,), jnp.bfloat16).at[target].set(route_weights.reshape(-1))
    )
    send_tokens = send_tokens.reshape(experts, capacity, model_width)
    send_cot = send_cot.reshape(experts, capacity, model_width)
    send_weight = send_weight.reshape(experts, capacity)
    recv_x, recv_cot, recv_weight = (
        lax.all_to_all(send_tokens, "ep", split_axis=0, concat_axis=1, tiled=True),
        lax.all_to_all(send_cot, "ep", split_axis=0, concat_axis=1, tiled=True),
        lax.all_to_all(send_weight, "ep", split_axis=0, concat_axis=1, tiled=True),
    )
    w_gate = weights[:, 0]
    w_up = weights[:, 1]
    w_down = weights[:, 2]
    gate_val = jnp.einsum("erd,edh->erh", recv_x, w_gate, preferred_element_type=jnp.float32)
    up_val = jnp.einsum("erd,edh->erh", recv_x, w_up, preferred_element_type=jnp.float32)
    sigmoid_gate = jax.nn.sigmoid(gate_val)
    activated = gate_val * sigmoid_gate
    hidden = lax.optimization_barrier((activated * up_val).astype(jnp.bfloat16))
    back_val = jnp.einsum("erd,edh->erh", recv_cot, w_down, preferred_element_type=jnp.float32)
    route_part = lax.optimization_barrier(
        jnp.sum(hidden.astype(jnp.float32) * back_val, 2).astype(jnp.bfloat16)
    )
    row_weight = recv_weight.astype(jnp.float32)[:, :, None]
    scaled = row_weight * back_val
    dgate = (scaled * up_val * sigmoid_gate * (1.0 + gate_val * (1.0 - sigmoid_gate))).astype(
        jnp.bfloat16
    )
    dup = (scaled * activated).astype(jnp.bfloat16)
    down_cot = (row_weight * recv_cot.astype(jnp.float32)).astype(jnp.bfloat16)
    slot_back = jnp.einsum("erh,edh->erd", dgate, w_gate, preferred_element_type=jnp.float32)
    slot_back = slot_back + jnp.einsum(
        "erh,edh->erd", dup, w_up, preferred_element_type=jnp.float32
    )
    slot_back = lax.optimization_barrier(slot_back.astype(jnp.bfloat16))
    ret_rows, ret_route = (
        lax.all_to_all(slot_back, "ep", split_axis=1, concat_axis=0, tiled=True),
        lax.all_to_all(route_part, "ep", split_axis=1, concat_axis=0, tiled=True),
    )
    picked = ret_rows.reshape(experts * capacity, model_width)[target]
    token_grad = jnp.sum(
        picked.reshape(tok_count, topk_count, model_width).astype(jnp.float32), 1
    ).astype(jnp.bfloat16)
    routing_grad = ret_route.reshape(-1)[target].reshape(tok_count, topk_count)
    grad_local = jnp.stack(
        [
            jnp.einsum("erd,erh->edh", recv_x, dgate, preferred_element_type=jnp.float32),
            jnp.einsum("erd,erh->edh", recv_x, dup, preferred_element_type=jnp.float32),
            jnp.einsum("erd,erh->edh", down_cot, hidden, preferred_element_type=jnp.float32),
        ],
        1,
    )
    grad_share = lax.psum_scatter(grad_local, "dp", scatter_dimension=2, tiled=True)
    square_sum = lax.psum(jnp.sum(grad_share * grad_share), ("dp", "ep"))
    param_count = 3.0 * experts * model_width * hidden_units
    root_mean = jnp.sqrt(square_sum / param_count + 1e-06)
    clip_factor = jnp.minimum(1.0, 0.5 / root_mean)
    clipped = clip_factor * grad_share
    first_next = 0.9 * first_moment.astype(jnp.float32) + 0.1 * clipped
    second_next = 0.95 * second_moment.astype(jnp.float32) + 0.05 * clipped * clipped
    update = (
        first_next
        / (1.0 - 0.9**ADAM_STEP)
        / (jnp.sqrt(second_next / (1.0 - 0.95**ADAM_STEP)) + 1e-08)
    )
    return (
        token_grad,
        routing_grad,
        first_next.astype(jnp.bfloat16),
        second_next.astype(jnp.bfloat16),
        update.astype(jnp.bfloat16),
    )


def finish(grad_share, square_sum, first_moment, second_moment, param_count):
    root_mean = jnp.sqrt(square_sum / param_count + 1e-06)
    clip_factor = jnp.minimum(1.0, 0.5 / root_mean)
    clipped = clip_factor * grad_share
    first_next = 0.9 * first_moment.astype(jnp.float32) + 0.1 * clipped
    second_next = 0.95 * second_moment.astype(jnp.float32) + 0.05 * clipped * clipped
    update = (
        first_next
        / (1.0 - 0.9**ADAM_STEP)
        / (jnp.sqrt(second_next / (1.0 - 0.95**ADAM_STEP)) + 1e-08)
    )
    return (
        first_next.astype(jnp.bfloat16),
        second_next.astype(jnp.bfloat16),
        update.astype(jnp.bfloat16),
    )


MESH = pl.DeviceIdType.MESH
MIB = 1024 * 1024


def place(groups):
    me = lax.axis_index("ep")
    core = lax.rem(me, 2)
    side = lax.rem(me // 2, 2)
    return me // 4, side, core, groups // 4


def index_of(z, y, core):
    return (z * 2 + y) * 2 + core


def greet(z, y, core, depth, partner):
    barrier = pltpu.get_barrier_semaphore()

    def hello(device):
        pl.semaphore_signal(barrier, inc=1, device_id=device, device_id_type=MESH)

    hello({"ep": index_of(z, y, 1 - core)})
    hello({"ep": index_of(z, 1 - y, core)})
    expected = 2
    if partner is not None:
        hello(partner)
        expected = 3

    for level in range(depth):
        @pl.when(z != level)
        def _():
            hello({"ep": index_of(level, y, core)})

    pl.semaphore_wait(barrier, expected + depth - 1)


def gather_kernel(groups, x_ref, c_ref, t_ref, xs, cs, ts, up_sem, down_sem, y_sem, core_sem, recv_sem, own_sem):
    z, y, core, depth = place(groups)
    me = index_of(z, y, core)
    arrays = ((x_ref, xs), (c_ref, cs), (t_ref, ts))
    greet(z, y, core, depth, None)

    above, below = index_of(z + 1, y, core), index_of(z - 1, y, core)
    beside, sibling = index_of(z, 1 - y, core), index_of(z, y, 1 - core)
    paired = z + 1 - 2 * lax.rem(z, 2)

    def copy(i, block, source_own, sems, slot, device):
        own, full = arrays[i]
        return pltpu.make_async_remote_copy(
            src_ref=own if source_own else full.at[block],
            dst_ref=full.at[block],
            send_sem=sems.at[i, slot],
            recv_sem=recv_sem.at[i, block],
            device_id={"ep": device},
            device_id_type=MESH,
        )

    def arrived(i, block):
        copy(i, block, False, core_sem, 0, sibling).wait_recv()

    local = [
        pltpu.make_async_copy(own, full.at[me], own_sem.at[i])
        for i, (own, full) in enumerate(arrays)
    ]
    for i in range(3):
        @pl.when(z < depth - 1)
        def _():
            copy(i, me, True, up_sem, z, above).start()

        @pl.when(z > 0)
        def _():
            copy(i, me, True, down_sem, z, below).start()

        copy(i, me, True, y_sem, z, beside).start()
        copy(i, me, True, core_sem, z * 2 + y, sibling).start()
    for each in local:
        each.start()

    def spread_column(i, level, onward, sems, device):
        block = index_of(level, y, core)
        arrived(i, block)

        @pl.when(onward)
        def _():
            copy(i, block, False, sems, level, device).start()

        if i == 1:
            @pl.when(level != paired)
            def _():
                copy(i, block, False, y_sem, level, beside).start()
        else:
            copy(i, block, False, y_sem, level, beside).start()
        copy(i, block, False, core_sem, level * 2 + y, sibling).start()

    for step in range(1, depth):
        for i in range(3):
            @pl.when(z - step >= 0)
            def _():
                spread_column(i, z - step, z < depth - 1, up_sem, above)

            @pl.when(z + step <= depth - 1)
            def _():
                spread_column(i, z + step, z > 0, down_sem, below)

        if step == 1:
            far = index_of(z, 1 - y, core)
            for i in range(3):
                arrived(i, far)
                if i == 1:
                    copy(i, far, False, y_sem, paired, index_of(paired, y, core)).start()
                copy(i, far, False, core_sem, z * 2 + 1 - y, sibling).start()

    def pass_on(level):
        far = index_of(level, 1 - y, core)
        for i in range(3):
            arrived(i, far)
            copy(i, far, False, core_sem, level * 2 + 1 - y, sibling).start()

    for step in range(1, depth):
        @pl.when(z - step >= 0)
        def _():
            pass_on(z - step)

        @pl.when(z + step <= depth - 1)
        def _():
            pass_on(z + step)

    for level in range(depth):
        for side in range(2):
            for i in range(3):
                arrived(i, index_of(level, side, 1 - core))
    for each in local:
        each.wait()

    def sent(sems, slot, device):
        for i in range(3):
            copy(i, me, True, sems, slot, device).wait_send()

    for level in range(depth):
        @pl.when((z < depth - 1) & (level <= z))
        def _():
            sent(up_sem, level, above)

        @pl.when((z > 0) & (level >= z))
        def _():
            sent(down_sem, level, below)

        sent(y_sem, level, beside)
        for side in range(2):
            sent(core_sem, level * 2 + side, sibling)


def gather_blocks(tokens, cotangent, table, groups):
    depth = groups // 4
    any_space = pl.BlockSpec(memory_space=pl.ANY)
    dma = pltpu.SemaphoreType.DMA
    arrays = (tokens, cotangent, table)
    return pl.pallas_call(
        functools.partial(gather_kernel, groups),
        out_shape=[jax.ShapeDtypeStruct((groups,) + a.shape, a.dtype) for a in arrays],
        in_specs=[any_space] * 3,
        out_specs=[any_space] * 3,
        scratch_shapes=[
            dma((3, depth)),
            dma((3, depth)),
            dma((3, depth)),
            dma((3, 2 * depth)),
            dma((3, groups)),
            dma((3,)),
        ],
        compiler_params=pltpu.CompilerParams(
            collective_id=1, has_side_effects=True, vmem_limit_bytes=48 * MIB
        ),
    )(*arrays)


def combine_kernel(
    groups, sp, rt, g0, g1, g2, k0, k1, k2, out, route_out, share_out, squares,
    g_got,
    core_s, core_r, ys_s, ys_r, y_s, y_r, zs_s, zs_r, in_s, in_r,
    core_send, core_recv, y_send, y_recv, z_send, z_recv, g_sem, n_out, n_in, n_send, n_recv,
):
    z, y, core, depth = place(groups)
    partner = {"dp": 1 - lax.axis_index("dp")}
    greet(z, y, core, depth, partner)
    g_copies = [
        pltpu.make_async_remote_copy(
            src_ref=g, dst_ref=g_got.at[i], send_sem=g_sem.at[0, i], recv_sem=g_sem.at[1, i],
            device_id=partner, device_id_type=MESH,
        )
        for i, g in enumerate((g0, g1, g2))
    ]
    for copy in g_copies:
        copy.start()
    kept = (k0, k1, k2)
    chunk = 16
    chunks = sp.shape[1] // chunk
    f32, bf16 = jnp.float32, jnp.bfloat16

    def target(j):
        if j == depth - 1:
            return z
        low = jnp.where(depth - 1 - j > z, depth - 1 - j, depth - 2 - j)
        high = jnp.where(j < z, j, j + 1)
        return jnp.where(z < depth // 2, low, high)

    def pair(src, src_at, dst, dst_at, send, send_at, recv, recv_at, device):
        return [
            pltpu.make_async_remote_copy(
                src_ref=src[i].at[src_at], dst_ref=dst[i].at[dst_at],
                send_sem=send.at[i, send_at], recv_sem=recv.at[i, recv_at],
                device_id={"ep": device}, device_id_type=MESH,
            )
            for i in range(2)
        ]

    def core_copy(level, side):
        slot = level * 2 + side
        return pair(
            (sp, rt), index_of(level, side, 1 - core), (core_s, core_r), slot,
            core_send, slot, core_recv, slot, index_of(z, y, 1 - core),
        )

    def y_copy(level):
        return pair(
            (ys_s, ys_r), level, (y_s, y_r), level,
            y_send, level, y_recv, level, index_of(z, 1 - y, core),
        )

    def z_copy(level, going, slot):
        return pair(
            (zs_s, zs_r), level, (in_s, in_r), slot,
            z_send, level, z_recv, slot, index_of(going, y, core),
        )

    def add(result, terms):
        def body(i, carry):
            rows = pl.ds(pl.multiple_of(i * chunk, chunk), chunk)
            total = terms[0][0][terms[0][2], rows, :].astype(f32)
            for term in terms[1:]:
                total = total + term[0][term[2], rows, :].astype(f32)
            if result[2] is None:
                result[0][rows, :] = total.astype(bf16)
            else:
                result[0][result[2], rows, :] = total.astype(bf16)
            return carry

        lax.fori_loop(0, chunks, body, 0)
        small = terms[0][1][terms[0][2]].astype(f32)
        for term in terms[1:]:
            small = small + term[1][term[2]].astype(f32)
        if result[2] is None:
            result[1][...] = small.astype(bf16)
        else:
            result[1][result[2]] = small.astype(bf16)

    def each(copies, what):
        for copy in copies:
            getattr(copy, what)()

    for side in (1 - y, y):
        for j in range(depth):
            each(core_copy(target(j), side), "start")
    for j in range(depth):
        t = target(j)
        each(core_copy(t, 1 - y), "wait_recv")
        add((ys_s, ys_r, t), [(sp, rt, index_of(t, 1 - y, core)), (core_s, core_r, t * 2 + 1 - y)])
        each(y_copy(t), "start")
    for j in range(depth - 1):
        t = target(j)
        each(core_copy(t, y), "wait_recv")
        each(y_copy(t), "wait_recv")
        terms = [(sp, rt, index_of(t, y, core)), (core_s, core_r, t * 2 + y), (y_s, y_r, t)]
        upward = t > z
        slot = jnp.where(upward, t, depth + t)
        going = jnp.where(upward, z + 1, z - 1)
        more = (upward & (z > 0)) | (jnp.logical_not(upward) & (z < depth - 1))

        @pl.when(more)
        def _():
            each(z_copy(t, going, slot), "wait_recv")
            add((zs_s, zs_r, t), terms + [(in_s, in_r, slot)])

        @pl.when(jnp.logical_not(more))
        def _():
            add((zs_s, zs_r, t), terms)

        each(z_copy(t, going, slot), "start")
    for copy in g_copies:
        copy.wait()

    width, piece = k0.shape[1], 32

    def square(i, carry):
        rows = pl.ds(pl.multiple_of(i * piece, piece), piece)
        for unit in range(3):
            share = kept[unit][rows, :] + g_got[unit, rows, :].astype(f32)
            share_out[unit, rows, :] = share
            carry = carry + share * share
        return carry

    sums = lax.fori_loop(0, k0.shape[0] // piece, square, jnp.zeros((piece, width), f32))
    sums = sum(sums[i * 8:(i + 1) * 8] for i in range(piece // 8))
    sums = sum(sums[:, i * 128:(i + 1) * 128] for i in range(width // 128))

    def share_sum(src, dst, device, recv):
        return pltpu.make_async_remote_copy(
            src_ref=n_out.at[src], dst_ref=n_in.at[dst], send_sem=n_send.at[recv],
            recv_sem=n_recv.at[dst], device_id=device, device_id_type=MESH,
        )

    for stage, device in enumerate(
        (partner, {"ep": index_of(z, y, 1 - core)}, {"ep": index_of(z, 1 - y, core)})
    ):
        n_out[stage] = sums
        trade = share_sum(stage, stage, device, stage)
        trade.start()
        trade.wait()
        sums = sums + n_in[stage]
    n_out[3] = sums
    for level in range(depth):
        @pl.when(z != level)
        def _():
            share_sum(3, 3 + z, {"ep": index_of(level, y, core)}, 3 + level).start()

    squares[...] = sums
    for level in range(depth):
        @pl.when(z != level)
        def _():
            share_sum(3, 3 + level, {"ep": index_of(level, y, core)}, 3 + level).wait()
            squares[...] += n_in[3 + level]
    each(core_copy(z, y), "wait_recv")
    each(y_copy(z), "wait_recv")
    terms = [(sp, rt, index_of(z, y, core)), (core_s, core_r, z * 2 + y), (y_s, y_r, z)]
    from_below, from_above = (in_s, in_r, z), (in_s, in_r, depth + z)
    beside = jnp.where(z > 0, z - 1, z + 1)

    @pl.when(z > 0)
    def _():
        each(z_copy(z, beside, z), "wait_recv")

    @pl.when(z < depth - 1)
    def _():
        each(z_copy(z, beside, depth + z), "wait_recv")

    @pl.when((z > 0) & (z < depth - 1))
    def _():
        add((out, route_out, None), terms + [from_below, from_above])

    @pl.when(z == 0)
    def _():
        add((out, route_out, None), terms + [from_above])

    @pl.when(z == depth - 1)
    def _():
        add((out, route_out, None), terms + [from_below])

    for j in range(depth):
        t = target(j)
        each(core_copy(t, 0), "wait_send")
        each(core_copy(t, 1), "wait_send")
        each(y_copy(t), "wait_send")
        if j < depth - 1:
            each(z_copy(t, beside, t), "wait_send")


def combine(spread, routes, sent, kept, groups):
    depth = groups // 4
    bf16 = jnp.bfloat16
    big, small = spread.shape[1:], routes.shape[1:]
    vmem, any_space = pl.BlockSpec(memory_space=pltpu.VMEM), pl.BlockSpec(memory_space=pl.ANY)
    dma = pltpu.SemaphoreType.DMA

    def both(count):
        return [pltpu.VMEM((count,) + big, bf16), pltpu.VMEM((count,) + small, bf16)]

    return pl.pallas_call(
        functools.partial(combine_kernel, groups),
        out_shape=[
            jax.ShapeDtypeStruct(big, bf16),
            jax.ShapeDtypeStruct(small, bf16),
            jax.ShapeDtypeStruct((3,) + kept[0].shape, jnp.float32),
            jax.ShapeDtypeStruct((8, 128), jnp.float32),
        ],
        in_specs=[vmem] * 2 + [any_space] * 3 + [vmem] * 3,
        out_specs=[vmem, vmem, vmem, vmem],
        scratch_shapes=[pltpu.VMEM((3,) + kept[0].shape, bf16)] + both(2 * depth) + both(depth) + both(depth) + both(depth) + both(2 * depth)
        + [
            dma((2, 2 * depth)), dma((2, 2 * depth)),
            dma((2, depth)), dma((2, depth)),
            dma((2, depth)), dma((2, 2 * depth)),
            dma((2, 3)),
            pltpu.VMEM((4, 8, 128), jnp.float32),
            pltpu.VMEM((3 + depth, 8, 128), jnp.float32),
            dma((3 + depth,)),
            dma((3 + depth,)),
        ],
        compiler_params=pltpu.CompilerParams(
            collective_id=2, has_side_effects=True, vmem_limit_bytes=52 * MIB
        ),
    )(spread, routes, *sent, *kept)


def on_device_gather(
    tokens, cotangent, expert_ids, route_weights, weights, first_moment, second_moment
):
    f32, bf16 = jnp.float32, jnp.bfloat16
    tok_count, model_width = tokens.shape
    topk_count = expert_ids.shape[1]
    hidden_units = weights.shape[3]
    groups = lax.axis_size("ep")
    experts = groups
    capacity = (tok_count * topk_count * 9 + 8 * experts - 1) // (8 * experts)
    rows = groups * capacity
    named = expert_ids[:, :, None] == jnp.arange(experts, dtype=jnp.int32)[None, None, :]
    table = jnp.sum(jnp.where(named, route_weights.astype(f32)[:, :, None], 0.0), 1).T.astype(bf16)
    x_all, cot_all, tables = gather_blocks(tokens, cotangent, table, groups)
    me = lax.axis_index("ep")
    mine = lax.dynamic_slice_in_dim(tables, me, 1, 1)[:, 0, :]
    routed = mine > 0
    position = jnp.cumsum(routed.astype(jnp.int32), 1) - 1
    slots = jnp.arange(capacity, dtype=jnp.int32)
    pick = ((position[:, None, :] == slots[None, :, None]) & routed[:, None, :]).astype(bf16)
    recv_x = jnp.einsum("bst,btd->bsd", pick, x_all, preferred_element_type=f32).astype(bf16)
    recv_cot = jnp.einsum("bst,btd->bsd", pick, cot_all, preferred_element_type=f32).astype(bf16)
    recv_weight = jnp.sum(pick.astype(f32) * mine.astype(f32)[:, None, :], 2)
    recv_x = recv_x.reshape(rows, model_width)
    recv_cot = recv_cot.reshape(rows, model_width)
    row_weight = recv_weight.reshape(rows, 1)
    w_gate, w_up, w_down = weights[0, 0], weights[0, 1], weights[0, 2]
    gate_val = jnp.dot(recv_x, w_gate, preferred_element_type=f32)
    up_val = jnp.dot(recv_x, w_up, preferred_element_type=f32)
    sigmoid_gate = jax.nn.sigmoid(gate_val)
    activated = gate_val * sigmoid_gate
    hidden = lax.optimization_barrier((activated * up_val).astype(bf16))
    back_val = jnp.dot(recv_cot, w_down, preferred_element_type=f32)
    route_part = jnp.sum(hidden.astype(f32) * back_val, 1).astype(bf16)
    scaled = row_weight * back_val
    dgate = (scaled * up_val * sigmoid_gate * (1.0 + gate_val * (1.0 - sigmoid_gate))).astype(bf16)
    dup = (scaled * activated).astype(bf16)
    down_cot = (row_weight * recv_cot.astype(f32)).astype(bf16)
    by_row = (((0,), (0,)), ((), ()))
    half = model_width // 2
    part = lax.axis_index("dp")

    def grads(owner, kind):
        columns = lambda a: lax.dynamic_slice_in_dim(a, owner * half, half, 1)
        return [
            lax.dot_general(columns(rows_of), by, by_row, preferred_element_type=f32).astype(kind)
            for rows_of, by in ((recv_x, dgate), (recv_x, dup), (down_cot, hidden))
        ]

    sent, kept = grads(1 - part, bf16), grads(part, f32)
    by_col = (((1,), (1,)), ((), ()))
    slot_back = lax.dot_general(dgate, w_gate, by_col, preferred_element_type=f32)
    slot_back = slot_back + lax.dot_general(dup, w_up, by_col, preferred_element_type=f32)
    slot_back = slot_back.astype(bf16).reshape(groups, capacity, model_width)
    spread = jnp.einsum("bst,bsd->btd", pick, slot_back, preferred_element_type=f32).astype(bf16)
    route_rows = jnp.sum(
        pick.astype(f32) * route_part.astype(f32).reshape(groups, capacity, 1), 1
    )
    my_row = jnp.arange(experts, dtype=jnp.int32)[None, :, None] == me
    routes = jnp.where(my_row, route_rows[:, None, :], 0.0).astype(bf16)
    token_grad, route_back, share, squares = combine(spread, routes, sent, kept, groups)
    routing_grad = jnp.sum(
        jnp.where(named, route_back.T.astype(f32)[:, None, :], 0.0), 2
    ).astype(bf16)
    return (token_grad, routing_grad) + finish(
        share[None],
        jnp.sum(squares),
        first_moment,
        second_moment,
        3.0 * experts * model_width * hidden_units,
    )


def fits(mesh):
    return mesh.shape["dp"] == 2 and mesh.shape["ep"] == 16


def solution(mesh):
    in_specs = (
        P(("dp", "ep"), None),
        P(("dp", "ep"), None),
        P(("dp", "ep"), None),
        P(("dp", "ep"), None),
        P("ep", None, None, None),
        P("ep", None, "dp", None),
        P("ep", None, "dp", None),
    )
    out_specs = (
        P(("dp", "ep"), None),
        P(("dp", "ep"), None),
        P("ep", None, "dp", None),
        P("ep", None, "dp", None),
        P("ep", None, "dp", None),
    )
    return jax.shard_map(
        on_device_gather if fits(mesh) else on_device, mesh=mesh, in_specs=in_specs, out_specs=out_specs, check_vma=False
    )
```
